512 devices in a mesh: user: 8 (over x, core), seq: 64 (over z, y).
Axes of the slice: x: 4, y: 4, z: 16, core: 2. Of those that a mesh axis runs over, the one named last changes fastest.
Arguments:
- kv_cache: bfloat16 [16, 8192, 2, 2, 512], P('user', 'seq'), may hold values from -6 to 6
- spill_cache: bfloat16 [8, 4096, 2, 2, 512], P('user', 'seq'), may hold values from -6 to 6
- spill_owner: int32 [8, 64], P('user', 'seq'), may hold values from 0 to 1, as said below
- lengths: int32 [16], P('user'), may hold values from 2048 to 8192, as said below
- beam_tokens: int32 [16, 8, 4], P('user'), may hold values from 0 to 255
- codebook_embed: bfloat16 [4, 256, 512], P(None, 'user'), may hold values from -6 to 6
- w_query: bfloat16 [2, 512, 512], replicated, may hold values from -0.25 to 0.25
- w_gate: bfloat16 [2, 512, 512], replicated, may hold values from -0.25 to 0.25
- w_out: bfloat16 [2, 512, 512], replicated, may hold values from -0.25 to 0.25
Outputs:
- logits: float32 [16, 8, 4, 256], P('user')
The draws below stay inside these ranges and needn't reach their ends.
Inputs may be any that keep to these rules, and one draw needn't show every extreme that they name: `lengths`: lengths lie between 2048 and 8192; some user has length 8192. `spill_owner`: each value names a user of the group, as an index 0 to 1.
All inputs are finite; a program needn't handle non-finite values.
Results may differ from the reference program's by a relative error of at most 0.011.
Values may be sent and summed in bfloat16 or wider, within the bound.
No kernel may reach another device: no remote copies, remote signals or barrier semaphores. Data moves between devices by JAX's collectives and lax.ppermute only.
A program may use at most 64 MiB of HBM per device.

```python
import jax
import jax.numpy as jnp
from jax import lax

D = 512
H = 8
V = 256
LEVELS = 4
LAYERS = 2
BEAMS = 8
U_DEV = 2
SPILL = 64
HIST = 8192
USERS = 16
N_USER = 8
N_SEQ = 64


def draw_spill_owner(key, part):
    key = jax.random.fold_in(key, 2)
    first, second = jax.random.split(key)
    owners = jax.random.randint(first, (N_USER, N_SEQ), 0, U_DEV)
    coins = jax.random.randint(second, (N_USER, N_SEQ), 0, 2)
    owners = jnp.where(coins == 0, 0, owners)
    owners = owners.at[:, 0].set(U_DEV - 1)
    return owners.astype(jnp.int32)


def draw_lengths(key, part):
    key = jax.random.fold_in(key, 1)
    drawn = jax.random.randint(key, (USERS,), HIST // 4, HIST + 1)
    drawn = drawn.at[0].set(HIST)
    return drawn.astype(jnp.int32)


def with_ends(values, stream_key, smallest, largest):
    place = [jax.random.randint(jax.random.fold_in(stream_key, axis), (), 0, length) for axis, length in enumerate(values.shape)]
    main_axis = values.shape.index(max(values.shape))
    next_to = place[:main_axis] + [(place[main_axis] + 1) % values.shape[main_axis]] + place[main_axis + 1:]
    return values.at[tuple(place)].set(smallest).at[tuple(next_to)].set(largest)


def shard_levels(rng, extent, cuts, least, largest):
    def one(dim, blocks):
        heights = jax.random.uniform(jax.random.fold_in(jax.random.fold_in(rng, 6), dim), (blocks,), jnp.float32, least / len(cuts), largest / len(cuts))
        return jnp.repeat(jnp.exp(heights), extent[dim] // blocks).reshape((-1,) + (1,) * (len(extent) - dim - 1))

    gain = one(*cuts[0])
    for cut in cuts[1:]:
        gain = gain * one(*cut)
    return gain


def bell_draw(key, extent, spread, reach, cuts=(), kind=jnp.bfloat16):
    entries = jax.random.normal(key, extent, jnp.float32) * spread
    if len(cuts) > 0:
        entries = shard_levels(key, extent, cuts, -0.22, 0.18) * entries
    return jnp.clip(entries, min=-reach, max=reach).astype(kind)


def setup_inputs(seed: int = 0) -> dict:
    key_of = jax.random.split(jax.random.key(seed), 10)
    return {
        "kv_cache": bell_draw(key_of[0], (USERS, HIST, LAYERS, 2, D), 1.0, 6.0, ((0, 8), (1, 64))),
        "spill_cache": bell_draw(key_of[1], (N_USER, N_SEQ * SPILL, LAYERS, 2, D), 1.0, 6.0, ((0, 8), (1, 64))),
        "spill_owner": draw_spill_owner(jax.random.fold_in(key_of[9], 71), 0),
        "lengths": draw_lengths(jax.random.fold_in(key_of[9], 71), 0),
        "beam_tokens": with_ends(jax.random.randint(key_of[4], (USERS, BEAMS, LEVELS), 0, V), jax.random.fold_in(key_of[4], 1), 0, V - 1).astype(jnp.int32),
        "codebook_embed": bell_draw(key_of[5], (LEVELS, V, D), 1.0, 6.0, ((1, 8),)),
        "w_query": bell_draw(key_of[6], (LAYERS, D, D), D ** -0.5, 0.25),
        "w_gate": bell_draw(key_of[7], (LAYERS, D, D), D ** -0.5, 0.25),
        "w_out": bell_draw(key_of[8], (LAYERS, D, D), D ** -0.5, 0.25),
    }


EPSILON = 1e-06

def normalize(values):
    return values * lax.rsqrt(lax.optimization_barrier(jnp.mean(values * values, axis=-1, keepdims=True)) + EPSILON)

def cross_layer(stream, memory, keep, w_query, w_gate, w_out, layer):
    head_size = D // H
    normed = normalize(stream).astype(jnp.bfloat16)
    queries = jnp.dot(normed, w_query[layer], preferred_element_type=jnp.float32).astype(jnp.bfloat16)
    gate_act = jax.nn.silu(jnp.dot(normed, w_gate[layer], preferred_element_type=jnp.float32))
    query_heads = queries.reshape(BEAMS, H, head_size).astype(jnp.float32)
    key_heads = memory[:, layer, 0].reshape(-1, H, head_size).astype(jnp.float32)
    value_heads = memory[:, layer, 1].reshape(-1, H, head_size).astype(jnp.float32)
    scores = jnp.einsum('bhd,phd->bhp', query_heads, key_heads) * head_size ** (-0.5)
    weights_bf = (jax.nn.silu(scores) * keep[None, None, :]).astype(jnp.bfloat16)
    numerator = jnp.einsum('bhp,phd->bhd', weights_bf.astype(jnp.float32), value_heads).reshape(BEAMS, D)
    gated = (normalize(numerator) * gate_act).astype(jnp.bfloat16)
    return stream + jnp.dot(gated, w_out[layer], preferred_element_type=jnp.float32)

def reference(kv_cache, spill_cache, spill_owner, lengths, beam_tokens, codebook_embed, w_query, w_gate, w_out):
    kv_groups = kv_cache.reshape(N_USER, U_DEV, HIST, LAYERS, 2, D)
    len_groups = lengths.reshape(N_USER, U_DEV)
    tok_groups = beam_tokens.reshape(N_USER, U_DEV, BEAMS, LEVELS)

    def one_group(items):
        kv_group, len_group, tok_group, spill_group, owner_group = items
        spill_slots = owner_group[jnp.arange(N_SEQ * SPILL, dtype=jnp.int32) // SPILL]

        def one_user(inner):
            kv_user, len_user, tok_user, local = inner
            keep = jnp.concatenate([jnp.arange(HIST, dtype=jnp.int32) < len_user, spill_slots == local]).astype(jnp.float32)
            memory = jnp.concatenate([kv_user, spill_group], axis=0)
            stream = jnp.zeros((BEAMS, D), jnp.float32)
            outputs = []
            for level in range(LEVELS):
                onehot = (tok_user[:, level][:, None] == jnp.arange(V, dtype=jnp.int32)[None, :]).astype(jnp.bfloat16)
                stream = stream + jnp.dot(onehot, codebook_embed[level], preferred_element_type=jnp.float32)
                for layer in range(LAYERS):
                    stream = cross_layer(stream, memory, keep, w_query, w_gate, w_out, layer)
                final = normalize(stream).astype(jnp.bfloat16)
                outputs.append(jnp.dot(final, codebook_embed[level].T, preferred_element_type=jnp.float32) * D ** (-0.5))
            return jnp.stack(outputs, axis=1)
        return lax.map(one_user, (kv_group, len_group, tok_group, jnp.arange(U_DEV, dtype=jnp.int32)))
    result = lax.map(one_group, (kv_groups, len_groups, tok_groups, spill_cache, spill_owner))
    return result.reshape(USERS, BEAMS, LEVELS, V)
```

```python
import functools

import jax
import jax.numpy as jnp
from jax import lax
from jax.experimental import pallas as pl
from jax.experimental.pallas import tpu as pltpu
from jax.sharding import Mesh, PartitionSpec as P

D = 512
H = 8
V = 256
LEVELS = 4
LAYERS = 2
BEAMS = 8
U_DEV = 2
NX, NC, NZ, NY = 4, 2, 16, 4
GROUPS = NX * NC
PLANE = NX * NC * NY
COLS = D // NX
HEAD = D // H
EPSILON = 1e-06
PLANE_AXES = ("x", "core", "y")
USER_AXES = ("x", "core")

bf16 = jnp.bfloat16
f32 = jnp.float32


def normalize(values):
    return values * lax.rsqrt(jnp.mean(values * values, axis=-1, keepdims=True) + EPSILON)


def silu(values):
    return values / (1.0 + jnp.exp(-values))


def finish_layer(recv_ref, stream_ref, gate_ref, wo_ref):
    sums = jnp.sum(recv_ref[...].reshape(NX, NC * NY, BEAMS, COLS), axis=1)
    total = jnp.concatenate([sums[i] for i in range(NX)], axis=-1)
    gated = (normalize(total) * gate_ref[...]).astype(bf16)
    return stream_ref[...] + jnp.dot(gated, wo_ref[...], preferred_element_type=f32)


def begin_layer(stream, kv_ref, wq_ref, wg_ref, out_ref, gate_out):
    normed = normalize(stream).astype(bf16)
    query = jnp.dot(normed, wq_ref[...], preferred_element_type=f32)
    gate_out[...] = silu(jnp.dot(normed, wg_ref[...], preferred_element_type=f32))
    low = lax.broadcasted_iota(jnp.int32, (BEAMS, COLS), 1) < HEAD
    pair = jnp.concatenate([jnp.where(low, query, 0.0), jnp.where(low, 0.0, query)], axis=0)
    keys = kv_ref[:, 0].reshape(-1, COLS)
    values = kv_ref[:, 1].reshape(-1, COLS)
    scores = lax.dot_general(
        pair.astype(bf16), keys, (((1,), (1,)), ((), ())), preferred_element_type=f32
    ) * HEAD ** (-0.5)
    weights = silu(scores).astype(bf16)
    part = jnp.dot(weights, values, preferred_element_type=f32)
    mine = jnp.where(low, part[:BEAMS], part[BEAMS:])
    out_ref[...] = jnp.broadcast_to(mine[None], (PLANE, BEAMS, COLS))


def first_kernel(emb_ref, kv_ref, wq_ref, wg_ref, out_ref, stream_out, gate_out):
    stream = emb_ref[...]
    stream_out[...] = stream
    begin_layer(stream, kv_ref, wq_ref, wg_ref, out_ref, gate_out)


def middle_kernel(recv_ref, stream_ref, gate_ref, wo_ref, kv_ref, wq_ref, wg_ref, out_ref, stream_out, gate_out):
    stream = finish_layer(recv_ref, stream_ref, gate_ref, wo_ref)
    stream_out[...] = stream
    begin_layer(stream, kv_ref, wq_ref, wg_ref, out_ref, gate_out)


def level_logits(stream, table_ref):
    final = normalize(stream).astype(bf16)
    return lax.dot_general(
        final, table_ref[...], (((1,), (1,)), ((), ())), preferred_element_type=f32
    ) * D ** (-0.5)


def turn_kernel(recv_ref, stream_ref, gate_ref, wo_ref, kv_ref, wq_ref, wg_ref, emb_ref, table_ref,
                out_ref, stream_out, gate_out, logits_out):
    stream = finish_layer(recv_ref, stream_ref, gate_ref, wo_ref)
    logits_out[...] = level_logits(stream, table_ref)
    stream = stream + emb_ref[...]
    stream_out[...] = stream
    begin_layer(stream, kv_ref, wq_ref, wg_ref, out_ref, gate_out)


def last_kernel(recv_ref, stream_ref, gate_ref, wo_ref, table_ref, logits_out):
    stream = finish_layer(recv_ref, stream_ref, gate_ref, wo_ref)
    logits = level_logits(stream, table_ref)
    logits_out[...] = jnp.broadcast_to(logits[None], (NZ, BEAMS, V))


VMEM = pl.BlockSpec(memory_space=pltpu.VMEM)


def call(kernel, args, outs):
    return pl.pallas_call(
        kernel,
        in_specs=[VMEM] * len(args),
        out_specs=[VMEM] * len(outs),
        out_shape=[jax.ShapeDtypeStruct(shape, f32) for shape in outs],
        compiler_params=pltpu.CompilerParams(vmem_limit_bytes=32 * 1024 * 1024),
    )(*args)


STEP_OUTS = [(PLANE, BEAMS, COLS), (BEAMS, D), (BEAMS, D)]


def body(
    kv_cache, spill_cache, spill_owner, lengths, beam_tokens, codebook_embed, w_query, w_gate, w_out
):
    xi, ci = lax.axis_index("x"), lax.axis_index("core")
    zi, yi = lax.axis_index("z"), lax.axis_index("y")
    span = kv_cache.shape[1]
    spill = spill_cache.shape[1]

    table = lax.all_gather(codebook_embed, USER_AXES, axis=1, tiled=True)
    tokens = lax.all_gather(beam_tokens, USER_AXES, axis=0, tiled=True)

    positions = (zi * NY + yi) * span + jnp.arange(span, dtype=jnp.int32)
    valid = positions[None, :] < lengths[:, None]
    owned = jnp.arange(U_DEV, dtype=jnp.int32) == spill_owner[0, 0]
    keep = jnp.concatenate(
        [valid.reshape(U_DEV, NC, span // NC), jnp.broadcast_to(owned[:, None, None], (U_DEV, NC, spill // NC))],
        axis=2,
    )
    resident = kv_cache.reshape(U_DEV, NC, span // NC, LAYERS, 2, NX, COLS)
    extra = jnp.broadcast_to(
        spill_cache.reshape(1, NC, spill // NC, LAYERS, 2, NX, COLS),
        (U_DEV, NC, spill // NC, LAYERS, 2, NX, COLS),
    )
    memory = jnp.concatenate([resident, extra], axis=2)
    is_value = jnp.arange(2) == 1
    memory = jnp.where(
        keep[:, :, :, None, None, None, None] | is_value[None, None, None, None, :, None, None],
        memory,
        jnp.zeros((), bf16),
    )
    memory = memory.transpose(5, 1, 0, 3, 4, 2, 6)
    share = memory.shape[5]
    memory = memory.reshape(GROUPS, U_DEV, LAYERS, 2, share, COLS)
    memory = lax.all_to_all(memory, USER_AXES, 0, 0, tiled=True)
    memory = memory.reshape(NZ, LAYERS, 2, share, COLS)
    memory = lax.all_to_all(memory, "z", 0, 0, tiled=True)
    kv = [memory[:, layer] for layer in range(LAYERS)]

    mine = lax.dynamic_index_in_dim(tokens, zi, 0, keepdims=False)
    onehot = (mine.T[:, :, None] == jnp.arange(V, dtype=jnp.int32)[None, None, :]).astype(bf16)
    embeds = jnp.einsum("tbv,tvd->tbd", onehot, table, preferred_element_type=f32)

    wq = [lax.dynamic_slice(w_query[layer], (0, xi * COLS), (D, COLS)) for layer in range(LAYERS)]
    wg = [w_gate[layer] for layer in range(LAYERS)]
    wo = [w_out[layer] for layer in range(LAYERS)]

    def exchange(parts):
        return lax.all_to_all(parts, PLANE_AXES, 0, 0, tiled=True)

    early = []
    for level in range(LEVELS):
        if level == 0:
            parts, stream, gate = call(first_kernel, (embeds[0], kv[0], wq[0], wg[0]), STEP_OUTS)
        else:
            parts, stream, gate, logits = call(
                turn_kernel,
                (recv, stream, gate, wo[1], kv[0], wq[0], wg[0], embeds[level], table[level - 1]),
                STEP_OUTS + [(BEAMS, V)],
            )
            early.append(logits)
        recv = exchange(parts)
        parts, stream, gate = call(
            middle_kernel, (recv, stream, gate, wo[0], kv[1], wq[1], wg[1]), STEP_OUTS
        )
        recv = exchange(parts)
    (final,) = call(last_kernel, (recv, stream, gate, wo[1], table[LEVELS - 1]), [(NZ, BEAMS, V)])
    last = lax.all_to_all(final, "z", 0, 0, tiled=True)
    group = xi * NC + ci
    pieces = [
        lax.dynamic_slice_in_dim(lax.all_gather(value, "z", axis=0), group * U_DEV, U_DEV, 0)
        for value in early
    ]
    pieces.append(lax.dynamic_slice_in_dim(last, group * U_DEV, U_DEV, 0))
    return jnp.stack(pieces, axis=2)


def solution(mesh):
    inner = Mesh(mesh.devices.reshape(NX, NC, NZ, NY), ("x", "core", "z", "y"))
    users, seq = ("x", "core"), ("z", "y")
    in_specs = (
        P(users, seq, None, None, None),
        P(users, seq, None, None, None),
        P(users, seq),
        P(users),
        P(users, None, None),
        P(None, users, None),
        P(),
        P(),
        P(),
    )
    out_specs = P(users, None, None, None)
    return jax.shard_map(body, mesh=inner, in_specs=in_specs, out_specs=out_specs, check_vma=False)
```

```python
import functools

import jax
import jax.numpy as jnp
from jax import lax
from jax.experimental import pallas as pl
from jax.experimental.pallas import tpu as pltpu
from jax.sharding import Mesh, PartitionSpec as P

D = 512
H = 8
V = 256
LEVELS = 4
LAYERS = 2
BEAMS = 8
U_DEV = 2
NX, NC, NQ, NL, NY = 4, 2, 4, 4, 4
AREA = NC * NL * NY
COLS = D // NC
HEAD = D // H
HEADS = COLS // HEAD
EPSILON = 1e-06
AREA_AXES = ("core", "zl", "y")
USER_AXES = ("x", "core")
Z_AXES = ("quad", "zl")
RINGS = [[NL * q + (i if q in (0, 3) else NL - 1 - i) for q in range(NQ)] for i in range(NL)]

bf16 = jnp.bfloat16
f32 = jnp.float32


def normalize(values):
    return values * lax.rsqrt(jnp.mean(values * values, axis=-1, keepdims=True) + EPSILON)


def silu(values):
    return values / (1.0 + jnp.exp(-values))


def finish_layer(layer, recv_ref, stream_ref, gate_ref, wo_ref):
    parts = recv_ref[...].astype(f32).reshape(NC, NL * NY, BEAMS, COLS)
    sums = jnp.sum(parts, axis=1)
    total = jnp.concatenate([sums[i] for i in range(NC)], axis=-1)
    gated = (normalize(total) * gate_ref[...]).astype(bf16)
    return stream_ref[...] + jnp.dot(gated, wo_ref[layer], preferred_element_type=f32)


def begin_layer(layer, stream, kv_ref, wq_ref, wg_ref, out_ref, gate_out):
    normed = normalize(stream).astype(bf16)
    query = jnp.dot(normed, wq_ref[layer], preferred_element_type=f32)
    gate_out[...] = silu(jnp.dot(normed, wg_ref[layer], preferred_element_type=f32))
    head_of = lax.broadcasted_iota(jnp.int32, (BEAMS, COLS), 1) // HEAD
    spread = jnp.concatenate([jnp.where(head_of == h, query, 0.0) for h in range(HEADS)], axis=0)
    keys = kv_ref[:, layer, 0].reshape(-1, COLS)
    values = kv_ref[:, layer, 1].reshape(-1, COLS)
    scores = lax.dot_general(
        spread.astype(bf16), keys, (((1,), (1,)), ((), ())), preferred_element_type=f32
    ) * HEAD ** (-0.5)
    weights = silu(scores).astype(bf16)
    part = jnp.dot(weights, values, preferred_element_type=f32)
    mine = jnp.zeros((BEAMS, COLS), f32)
    for h in range(HEADS):
        mine = jnp.where(head_of == h, part[h * BEAMS:(h + 1) * BEAMS], mine)
    copies = jnp.broadcast_to(mine[None], (AREA, BEAMS, COLS)).reshape(AREA * BEAMS, COLS)
    out_ref[...] = copies.astype(bf16)


def level_logits(level, stream, table_ref):
    final = normalize(stream).astype(bf16)
    return lax.dot_general(
        final, table_ref[level], (((1,), (1,)), ((), ())), preferred_element_type=f32
    ) * D ** (-0.5)


def first_kernel(emb_ref, kv_ref, wq_ref, wg_ref, out_ref, stream_out, gate_out):
    stream = emb_ref[0]
    stream_out[...] = stream
    begin_layer(0, stream, kv_ref, wq_ref, wg_ref, out_ref, gate_out)


def middle_kernel(recv_ref, stream_ref, gate_ref, wo_ref, kv_ref, wq_ref, wg_ref, out_ref, stream_out, gate_out):
    stream = finish_layer(0, recv_ref, stream_ref, gate_ref, wo_ref)
    stream_out[...] = stream
    begin_layer(1, stream, kv_ref, wq_ref, wg_ref, out_ref, gate_out)


def turn_kernel(level, recv_ref, stream_ref, gate_ref, wo_ref, kv_ref, wq_ref, wg_ref, emb_ref, table_ref,
                out_ref, stream_out, gate_out, logits_out):
    stream = finish_layer(1, recv_ref, stream_ref, gate_ref, wo_ref)
    logits_out[...] = level_logits(level - 1, stream, table_ref)
    stream = stream + emb_ref[level]
    stream_out[...] = stream
    begin_layer(0, stream, kv_ref, wq_ref, wg_ref, out_ref, gate_out)


def last_kernel(recv_ref, stream_ref, gate_ref, wo_ref, table_ref, *rest):
    early, logits_out = rest[:-1], rest[-1]
    stream = finish_layer(1, recv_ref, stream_ref, gate_ref, wo_ref)
    logits = jnp.concatenate(
        [ref[...] for ref in early] + [level_logits(LEVELS - 1, stream, table_ref)], axis=-1
    )
    logits_out[...] = jnp.broadcast_to(logits[None], (NQ, BEAMS, LEVELS * V))


VMEM = pl.BlockSpec(memory_space=pltpu.VMEM)


def call(kernel, args, outs):
    return pl.pallas_call(
        kernel,
        in_specs=[VMEM] * len(args),
        out_specs=[VMEM] * len(outs),
        out_shape=[jax.ShapeDtypeStruct(shape, kind) for shape, kind in outs],
        compiler_params=pltpu.CompilerParams(vmem_limit_bytes=32 * 1024 * 1024),
    )(*args)


STEP_OUTS = [((AREA * BEAMS, COLS), bf16), ((BEAMS, D), f32), ((BEAMS, D), f32)]


def body(
    kv_cache, spill_cache, spill_owner, lengths, beam_tokens, codebook_embed, w_query, w_gate, w_out
):
    ci, qi = lax.axis_index("core"), lax.axis_index("quad")
    li, yi = lax.axis_index("zl"), lax.axis_index("y")
    span = kv_cache.shape[1]
    spill = spill_cache.shape[1]

    table = lax.all_gather(codebook_embed, USER_AXES, axis=1, tiled=True)
    tokens = lax.all_gather(beam_tokens, "core", axis=0, tiled=True)

    positions = ((qi * NL + li) * NY + yi) * span + jnp.arange(span, dtype=jnp.int32)
    valid = positions[None, :] < lengths[:, None]
    owned = jnp.arange(U_DEV, dtype=jnp.int32) == spill_owner[0, 0]
    keep = jnp.concatenate([valid, jnp.broadcast_to(owned[:, None], (U_DEV, spill))], axis=1)
    resident = kv_cache.reshape(U_DEV, span, LAYERS, 2, NC, COLS)
    extra = jnp.broadcast_to(
        spill_cache.reshape(1, spill, LAYERS, 2, NC, COLS), (U_DEV, spill, LAYERS, 2, NC, COLS)
    )
    memory = jnp.concatenate([resident, extra], axis=1)
    is_value = jnp.arange(2) == 1
    memory = jnp.where(
        keep[:, :, None, None, None, None] | is_value[None, None, None, :, None, None],
        memory,
        jnp.zeros((), bf16),
    )
    memory = memory.transpose(4, 0, 2, 3, 1, 5)
    memory = lax.all_to_all(memory, "core", 0, 0, tiled=True)
    memory = memory.reshape(NQ, LAYERS, 2, span + spill, COLS)
    memory = lax.all_to_all(memory, Z_AXES, 0, 0, axis_index_groups=RINGS, tiled=True)

    mine = lax.dynamic_index_in_dim(tokens, qi, 0, keepdims=False)
    onehot = (mine.T[:, :, None] == jnp.arange(V, dtype=jnp.int32)[None, None, :]).astype(bf16)
    embeds = jnp.einsum("tbv,tvd->tbd", onehot, table, preferred_element_type=f32)
    wq = lax.dynamic_slice_in_dim(w_query, ci * COLS, COLS, 2)

    def exchange(parts):
        return lax.all_to_all(parts, AREA_AXES, 0, 0, tiled=True)

    early = []
    for level in range(LEVELS):
        if level == 0:
            parts, stream, gate = call(first_kernel, (embeds, memory, wq, w_gate), STEP_OUTS)
        else:
            parts, stream, gate, logits = call(
                functools.partial(turn_kernel, level),
                (recv, stream, gate, w_out, memory, wq, w_gate, embeds, table),
                STEP_OUTS + [((BEAMS, V), f32)],
            )
            early.append(logits)
        recv = exchange(parts)
        parts, stream, gate = call(
            middle_kernel, (recv, stream, gate, w_out, memory, wq, w_gate), STEP_OUTS
        )
        recv = exchange(parts)
    (logits,) = call(
        last_kernel, (recv, stream, gate, w_out, table, *early), [((NQ, BEAMS, LEVELS * V), f32)]
    )
    logits = lax.all_to_all(logits, Z_AXES, 0, 0, axis_index_groups=RINGS, tiled=True)
    logits = lax.dynamic_slice_in_dim(logits, ci * U_DEV, U_DEV, 0)
    return logits.reshape(U_DEV, BEAMS, LEVELS, V)


def solution(mesh):
    inner = Mesh(
        mesh.devices.reshape(NX, NC, NQ, NL, NY), ("x", "core", "quad", "zl", "y")
    )
    users, seq = ("x", "core"), ("quad", "zl", "y")
    in_specs = (
        P(users, seq, None, None, None),
        P(users, seq, None, None, None),
        P(users, seq),
        P(users),
        P(users, None, None),
        P(None, users, None),
        P(),
        P(),
        P(),
    )
    out_specs = P(users, None, None, None)
    return jax.shard_map(body, mesh=inner, in_specs=in_specs, out_specs=out_specs, check_vma=False)
```

```python
import functools

import jax
import jax.numpy as jnp
from jax import lax
from jax.experimental import pallas as pl
from jax.experimental.pallas import tpu as pltpu
from jax.sharding import Mesh, PartitionSpec as P

D = 512
H = 8
V = 256
LEVELS = 4
LAYERS = 2
BEAMS = 8
U_DEV = 2
NX, NC, NQ, NL, NY = 4, 2, 4, 4, 4
AREA = NC * NL * NY
COLS = D // NC
HEAD = D // H
HEADS = COLS // HEAD
EPSILON = 1e-06
AREA_AXES = ("core", "zl", "y")
USER_AXES = ("x", "core")
Z_AXES = ("quad", "zl")
RINGS = [[NL * q + (i if q in (0, 3) else NL - 1 - i) for q in range(NQ)] for i in range(NL)]

bf16 = jnp.bfloat16
f32 = jnp.float32


def normalize(values):
    return values * lax.rsqrt(jnp.mean(values * values, axis=-1, keepdims=True) + EPSILON)


def silu(values):
    return values / (1.0 + jnp.exp(-values))


def finish_layer(layer, recv_ref, stream_ref, gate_ref, wo_ref):
    parts = recv_ref[...].astype(f32).reshape(NC, NL * NY, BEAMS, COLS)
    sums = jnp.sum(parts, axis=1)
    total = jnp.concatenate([sums[i] for i in range(NC)], axis=-1)
    gated = (normalize(total) * gate_ref[...]).astype(bf16)
    return stream_ref[...] + jnp.dot(gated, wo_ref[layer], preferred_element_type=f32)


def begin_layer(layer, stream, kv_ref, wq_ref, wg_ref, out_ref, gate_out):
    normed = normalize(stream).astype(bf16)
    query = jnp.dot(normed, wq_ref[layer], preferred_element_type=f32)
    if wg_ref is not None:
        gate_out[...] = silu(jnp.dot(normed, wg_ref[layer], preferred_element_type=f32))
    head_of = lax.broadcasted_iota(jnp.int32, (BEAMS, COLS), 1) // HEAD
    spread = jnp.concatenate([jnp.where(head_of == h, query, 0.0) for h in range(HEADS)], axis=0)
    keys = kv_ref[:, layer, 0].reshape(-1, COLS)
    values = kv_ref[:, layer, 1].reshape(-1, COLS)
    scores = lax.dot_general(
        spread.astype(bf16), keys, (((1,), (1,)), ((), ())), preferred_element_type=f32
    ) * HEAD ** (-0.5)
    weights = silu(scores).astype(bf16)
    part = jnp.dot(weights, values, preferred_element_type=f32)
    mine = jnp.zeros((BEAMS, COLS), f32)
    for h in range(HEADS):
        mine = jnp.where(head_of == h, part[h * BEAMS:(h + 1) * BEAMS], mine)
    copies = jnp.broadcast_to(mine[None], (AREA, BEAMS, COLS)).reshape(AREA * BEAMS, COLS)
    out_ref[...] = copies.astype(bf16)


def level_logits(level, stream, table_ref):
    final = normalize(stream).astype(bf16)
    return lax.dot_general(
        final, table_ref[level], (((1,), (1,)), ((), ())), preferred_element_type=f32
    ) * D ** (-0.5)


def gate_kernel(emb_ref, wg_ref, wo_ref, gate_out):
    normed = normalize(emb_ref[0]).astype(bf16)
    gate_out[...] = silu(jnp.dot(normed, wg_ref[0], preferred_element_type=f32))


def first_kernel(emb_ref, gate_ref, kv_ref, wq_ref, out_ref, stream_out, gate_out):
    stream = emb_ref[0]
    stream_out[...] = stream
    gate_out[...] = gate_ref[...]
    begin_layer(0, stream, kv_ref, wq_ref, None, out_ref, None)


def middle_kernel(recv_ref, stream_ref, gate_ref, wo_ref, kv_ref, wq_ref, wg_ref, out_ref, stream_out, gate_out):
    stream = finish_layer(0, recv_ref, stream_ref, gate_ref, wo_ref)
    stream_out[...] = stream
    begin_layer(1, stream, kv_ref, wq_ref, wg_ref, out_ref, gate_out)


def turn_kernel(level, recv_ref, stream_ref, gate_ref, wo_ref, kv_ref, wq_ref, wg_ref, emb_ref, table_ref,
                out_ref, stream_out, gate_out, logits_out):
    stream = finish_layer(1, recv_ref, stream_ref, gate_ref, wo_ref)
    logits_out[...] = level_logits(level - 1, stream, table_ref)
    stream = stream + emb_ref[level]
    stream_out[...] = stream
    begin_layer(0, stream, kv_ref, wq_ref, wg_ref, out_ref, gate_out)


def last_kernel(recv_ref, stream_ref, gate_ref, wo_ref, table_ref, *rest):
    early, logits_out = rest[:-1], rest[-1]
    stream = finish_layer(1, recv_ref, stream_ref, gate_ref, wo_ref)
    logits = jnp.concatenate(
        [ref[...] for ref in early] + [level_logits(LEVELS - 1, stream, table_ref)], axis=-1
    )
    logits_out[...] = jnp.broadcast_to(logits[None], (NQ, BEAMS, LEVELS * V)).astype(bf16)


VMEM = pl.BlockSpec(memory_space=pltpu.VMEM)


def call(kernel, args, outs):
    return pl.pallas_call(
        kernel,
        in_specs=[VMEM] * len(args),
        out_specs=[VMEM] * len(outs),
        out_shape=[jax.ShapeDtypeStruct(shape, kind) for shape, kind in outs],
        compiler_params=pltpu.CompilerParams(vmem_limit_bytes=32 * 1024 * 1024),
    )(*args)


STEP_OUTS = [((AREA * BEAMS, COLS), bf16), ((BEAMS, D), f32), ((BEAMS, D), f32)]


def body(
    kv_cache, spill_cache, spill_owner, lengths, beam_tokens, codebook_embed, w_query, w_gate, w_out
):
    ci, qi = lax.axis_index("core"), lax.axis_index("quad")
    li, yi = lax.axis_index("zl"), lax.axis_index("y")
    span = kv_cache.shape[1]
    spill = spill_cache.shape[1]

    table = lax.all_gather(codebook_embed, USER_AXES, axis=1, tiled=True)
    tokens = lax.all_gather(beam_tokens, "core", axis=0, tiled=True)

    positions = ((qi * NL + li) * NY + yi) * span + jnp.arange(span, dtype=jnp.int32)
    valid = positions[None, :] < lengths[:, None]
    owned = jnp.arange(U_DEV, dtype=jnp.int32) == spill_owner[0, 0]
    keep = jnp.concatenate([valid, jnp.broadcast_to(owned[:, None], (U_DEV, spill))], axis=1)
    resident = kv_cache.reshape(U_DEV, span, LAYERS, 2, NC, COLS)
    extra = jnp.broadcast_to(
        spill_cache.reshape(1, spill, LAYERS, 2, NC, COLS), (U_DEV, spill, LAYERS, 2, NC, COLS)
    )
    memory = jnp.concatenate([resident, extra], axis=1)
    is_value = jnp.arange(2) == 1
    memory = jnp.where(
        keep[:, :, None, None, None, None] | is_value[None, None, None, :, None, None],
        memory,
        jnp.zeros((), bf16),
    )
    memory = memory.transpose(4, 0, 2, 3, 1, 5)
    memory = lax.all_to_all(memory, "core", 0, 0, tiled=True)
    memory = memory.reshape(NQ, LAYERS, 2, span + spill, COLS)
    memory = lax.all_to_all(memory, Z_AXES, 0, 0, axis_index_groups=RINGS, tiled=True)

    mine = lax.dynamic_index_in_dim(tokens, qi, 0, keepdims=False)
    onehot = (mine.T[:, :, None] == jnp.arange(V, dtype=jnp.int32)[None, None, :]).astype(bf16)
    embeds = jnp.einsum("tbv,tvd->tbd", onehot, table, preferred_element_type=f32)
    wq = lax.dynamic_slice_in_dim(w_query, ci * COLS, COLS, 2)

    def exchange(parts):
        return lax.all_to_all(parts, AREA_AXES, 0, 0, tiled=True)

    (early_gate,) = call(gate_kernel, (embeds, w_gate, w_out), STEP_OUTS[2:])
    early = []
    for level in range(LEVELS):
        if level == 0:
            parts, stream, gate = call(first_kernel, (embeds, early_gate, memory, wq), STEP_OUTS)
        else:
            parts, stream, gate, logits = call(
                functools.partial(turn_kernel, level),
                (recv, stream, gate, w_out, memory, wq, w_gate, embeds, table),
                STEP_OUTS + [((BEAMS, V), f32)],
            )
            early.append(logits)
        recv = exchange(parts)
        parts, stream, gate = call(
            middle_kernel, (recv, stream, gate, w_out, memory, wq, w_gate), STEP_OUTS
        )
        recv = exchange(parts)
    (logits,) = call(
        last_kernel, (recv, stream, gate, w_out, table, *early), [((NQ, BEAMS, LEVELS * V), bf16)]
    )
    logits = lax.all_to_all(logits, Z_AXES, 0, 0, axis_index_groups=RINGS, tiled=True)
    logits = lax.dynamic_slice_in_dim(logits, ci * U_DEV, U_DEV, 0)
    return logits.astype(f32).reshape(U_DEV, BEAMS, LEVELS, V)


def solution(mesh):
    inner = Mesh(
        mesh.devices.reshape(NX, NC, NQ, NL, NY), ("x", "core", "quad", "zl", "y")
    )
    users, seq = ("x", "core"), ("quad", "zl", "y")
    in_specs = (
        P(users, seq, None, None, None),
        P(users, seq, None, None, None),
        P(users, seq),
        P(users),
        P(users, None, None),
        P(None, users, None),
        P(),
        P(),
        P(),
    )
    out_specs = P(users, None, None, None)
    return jax.shard_map(body, mesh=inner, in_specs=in_specs, out_specs=out_specs, check_vma=False)
```

```python
import functools

import jax
import jax.numpy as jnp
from jax import lax
from jax.experimental import pallas as pl
from jax.experimental.pallas import tpu as pltpu
from jax.sharding import Mesh, PartitionSpec as P

D = 512
H = 8
V = 256
LEVELS = 4
LAYERS = 2
BEAMS = 8
U_DEV = 2
NX, NC, NQ, NL, NY = 4, 2, 4, 4, 4
AREA = NC * NL * NY
COLS = D // NC
HEAD = D // H
HEADS = COLS // HEAD
EPSILON = 1e-06
AREA_AXES = ("core", "zl", "y")
USER_AXES = ("x", "core")
Z_AXES = ("quad", "zl")
RINGS = [[NL * q + (i if q in (0, 3) else NL - 1 - i) for q in range(NQ)] for i in range(NL)]

bf16 = jnp.bfloat16
f32 = jnp.float32


def normalize(values):
    return values * lax.rsqrt(jnp.mean(values * values, axis=-1, keepdims=True) + EPSILON)


def silu(values):
    return values / (1.0 + jnp.exp(-values))


def finish_layer(layer, recv_ref, stream_ref, gate_ref, wo_ref):
    parts = recv_ref[...].astype(f32).reshape(NC, NL * NY, BEAMS, COLS)
    sums = jnp.sum(parts, axis=1)
    total = jnp.concatenate([sums[i] for i in range(NC)], axis=-1)
    gated = (normalize(total) * gate_ref[...]).astype(bf16)
    return stream_ref[...] + jnp.dot(gated, wo_ref[layer], preferred_element_type=f32)


def begin_layer(layer, stream, kv_ref, wq_ref, wg_ref, out_ref, gate_out):
    normed = normalize(stream).astype(bf16)
    query = jnp.dot(normed, wq_ref[layer], preferred_element_type=f32)
    if wg_ref is not None:
        gate_out[...] = silu(jnp.dot(normed, wg_ref[layer], preferred_element_type=f32))
    head_of = lax.broadcasted_iota(jnp.int32, (BEAMS, COLS), 1) // HEAD
    spread = jnp.concatenate([jnp.where(head_of == h, query, 0.0) for h in range(HEADS)], axis=0)
    keys = kv_ref[:, layer, 0].reshape(-1, COLS)
    values = kv_ref[:, layer, 1].reshape(-1, COLS)
    scores = lax.dot_general(
        spread.astype(bf16), keys, (((1,), (1,)), ((), ())), preferred_element_type=f32
    ) * HEAD ** (-0.5)
    weights = silu(scores).astype(bf16)
    part = jnp.dot(weights, values, preferred_element_type=f32)
    mine = jnp.zeros((BEAMS, COLS), f32)
    for h in range(HEADS):
        mine = jnp.where(head_of == h, part[h * BEAMS:(h + 1) * BEAMS], mine)
    copies = jnp.broadcast_to(mine[None], (AREA, BEAMS, COLS)).reshape(AREA * BEAMS, COLS)
    out_ref[...] = copies.astype(bf16)


def level_logits(level, stream, table_ref):
    final = normalize(stream).astype(bf16)
    return lax.dot_general(
        final, table_ref[level], (((1,), (1,)), ((), ())), preferred_element_type=f32
    ) * D ** (-0.5)


def gate_kernel(emb_ref, wg_ref, wo_ref, gate_out):
    normed = normalize(emb_ref[0]).astype(bf16)
    gate_out[...] = silu(jnp.dot(normed, wg_ref[0], preferred_element_type=f32))


def first_kernel(emb_ref, gate_ref, kv_ref, wq_ref, out_ref, stream_out, gate_out):
    stream = emb_ref[0]
    stream_out[...] = stream
    gate_out[...] = gate_ref[...]
    begin_layer(0, stream, kv_ref, wq_ref, None, out_ref, None)


def middle_kernel(recv_ref, stream_ref, gate_ref, wo_ref, kv_ref, wq_ref, wg_ref, out_ref, stream_out, gate_out):
    stream = finish_layer(0, recv_ref, stream_ref, gate_ref, wo_ref)
    stream_out[...] = stream
    begin_layer(1, stream, kv_ref, wq_ref, wg_ref, out_ref, gate_out)


def turn_kernel(level, recv_ref, stream_ref, gate_ref, wo_ref, kv_ref, wq_ref, wg_ref, emb_ref, table_ref,
                out_ref, stream_out, gate_out, logits_out):
    stream = finish_layer(1, recv_ref, stream_ref, gate_ref, wo_ref)
    logits_out[...] = level_logits(level - 1, stream, table_ref)
    stream = stream + emb_ref[level]
    stream_out[...] = stream
    begin_layer(0, stream, kv_ref, wq_ref, wg_ref, out_ref, gate_out)


def last_kernel(recv_ref, stream_ref, gate_ref, wo_ref, table_ref, *rest):
    early, logits_out = rest[:-1], rest[-1]
    stream = finish_layer(1, recv_ref, stream_ref, gate_ref, wo_ref)
    levels = [ref[...] for ref in early] + [level_logits(LEVELS - 1, stream, table_ref)]
    logits = jnp.stack(levels, axis=1)
    logits_out[...] = jnp.broadcast_to(logits[None], (NQ, BEAMS, LEVELS, V)).astype(bf16)


VMEM = pl.BlockSpec(memory_space=pltpu.VMEM)


def call(kernel, args, outs):
    return pl.pallas_call(
        kernel,
        in_specs=[VMEM] * len(args),
        out_specs=[VMEM] * len(outs),
        out_shape=[jax.ShapeDtypeStruct(shape, kind) for shape, kind in outs],
        compiler_params=pltpu.CompilerParams(vmem_limit_bytes=32 * 1024 * 1024),
    )(*args)


STEP_OUTS = [((AREA * BEAMS, COLS), bf16), ((BEAMS, D), f32), ((BEAMS, D), f32)]


def body(
    kv_cache, spill_cache, spill_owner, lengths, beam_tokens, codebook_embed, w_query, w_gate, w_out
):
    ci, qi = lax.axis_index("core"), lax.axis_index("quad")
    li, yi = lax.axis_index("zl"), lax.axis_index("y")
    span = kv_cache.shape[1]
    spill = spill_cache.shape[1]

    table = lax.all_gather(codebook_embed, USER_AXES, axis=1, tiled=True)
    tokens = lax.all_gather(beam_tokens, "core", axis=0, tiled=True)

    positions = ((qi * NL + li) * NY + yi) * span + jnp.arange(span, dtype=jnp.int32)
    valid = positions[None, :] < lengths[:, None]
    owned = jnp.arange(U_DEV, dtype=jnp.int32) == spill_owner[0, 0]
    keep = jnp.concatenate([valid, jnp.broadcast_to(owned[:, None], (U_DEV, spill))], axis=1)
    resident = kv_cache.reshape(U_DEV, span, LAYERS, 2, NC, COLS)
    extra = jnp.broadcast_to(
        spill_cache.reshape(1, spill, LAYERS, 2, NC, COLS), (U_DEV, spill, LAYERS, 2, NC, COLS)
    )
    memory = jnp.concatenate([resident, extra], axis=1)
    is_value = jnp.arange(2) == 1
    memory = jnp.where(
        keep[:, :, None, None, None, None] | is_value[None, None, None, :, None, None],
        memory,
        jnp.zeros((), bf16),
    )
    memory = memory.transpose(4, 0, 2, 3, 1, 5)
    memory = lax.all_to_all(memory, "core", 0, 0, tiled=True)
    memory = memory.reshape(NQ, LAYERS, 2, span + spill, COLS)
    memory = lax.all_to_all(memory, Z_AXES, 0, 0, axis_index_groups=RINGS, tiled=True)

    mine = lax.dynamic_index_in_dim(tokens, qi, 0, keepdims=False)
    onehot = (mine.T[:, :, None] == jnp.arange(V, dtype=jnp.int32)[None, None, :]).astype(bf16)
    embeds = jnp.einsum("tbv,tvd->tbd", onehot, table, preferred_element_type=f32)
    wq = lax.dynamic_slice_in_dim(w_query, ci * COLS, COLS, 2)

    def exchange(parts):
        return lax.all_to_all(parts, AREA_AXES, 0, 0, tiled=True)

    (early_gate,) = call(gate_kernel, (embeds, w_gate, w_out), STEP_OUTS[2:])
    early = []
    for level in range(LEVELS):
        if level == 0:
            parts, stream, gate = call(first_kernel, (embeds, early_gate, memory, wq), STEP_OUTS)
        else:
            parts, stream, gate, logits = call(
                functools.partial(turn_kernel, level),
                (recv, stream, gate, w_out, memory, wq, w_gate, embeds, table),
                STEP_OUTS + [((BEAMS, V), f32)],
            )
            early.append(logits)
        recv = exchange(parts)
        parts, stream, gate = call(
            middle_kernel, (recv, stream, gate, w_out, memory, wq, w_gate), STEP_OUTS
        )
        recv = exchange(parts)
    (logits,) = call(
        last_kernel, (recv, stream, gate, w_out, table, *early), [((NQ, BEAMS, LEVELS, V), bf16)]
    )
    logits = lax.all_to_all(logits, Z_AXES, 0, 0, axis_index_groups=RINGS, tiled=True)
    logits = lax.dynamic_slice_in_dim(logits, ci * U_DEV, U_DEV, 0)
    return logits.astype(f32)


def solution(mesh):
    inner = Mesh(
        mesh.devices.reshape(NX, NC, NQ, NL, NY), ("x", "core", "quad", "zl", "y")
    )
    users, seq = ("x", "core"), ("quad", "zl", "y")
    in_specs = (
        P(users, seq, None, None, None),
        P(users, seq, None, None, None),
        P(users, seq),
        P(users),
        P(users, None, None),
        P(None, users, None),
        P(),
        P(),
        P(),
    )
    out_specs = P(users, None, None, None)
    return jax.shard_map(body, mesh=inner, in_specs=in_specs, out_specs=out_specs, check_vma=False)
```
